256 devices in a mesh: prompt: 4 (over x), resp: 8 (over z_hi, core), head: 8 (over y, z_lo).
Axes of the slice: x: 4, y: 4, z: 8 (z_hi: 4, z_lo: 2; z = z_hi * 2 + z_lo), core: 2. Of those that a mesh axis runs over, the one named last changes fastest.
Arguments:
- queries: bfloat16 [32, 512, 8192], P(('prompt', 'resp'), None, 'head'), parts along dimension 0, may hold values from -200 to 200
- resp_keys: bfloat16 [32, 512, 512], P(('prompt', 'resp'), None, 'head'), parts along dimension 0, may hold values from -6 to 6
- resp_values: bfloat16 [32, 512, 512], P(('prompt', 'resp'), None, 'head'), parts along dimension 0, may hold values from -6 to 6
- prefix_keys: bfloat16 [4096, 512], P(('prompt', 'resp', 'head')), parts along dimension 0, may hold values from -7 to 7
- prefix_values: bfloat16 [4096, 512], P(('prompt', 'resp', 'head')), parts along dimension 0, may hold values from -6 to 6
- out_grad: bfloat16 [32, 512, 8192], P(('prompt', 'resp'), None, 'head'), parts along dimension 0, may hold values from -6 to 6
- resp_len: int32 [32], P(('prompt', 'resp')), parts along dimension 0, may hold values from 1 to 512, 2560 in all
- prefix_len: int32 [4], P('prompt'), parts along dimension 0, may hold values from 512 to 1024
Outputs:
- attn_out: bfloat16 [32, 512, 8192], P(('prompt', 'resp'), None, 'head'), parts along dimension 0
- query_grad: bfloat16 [32, 512, 8192], P(('prompt', 'resp'), None, 'head'), parts along dimension 0
- resp_key_grad: float32 [32, 512, 512], P(('prompt', 'resp'), None, 'head'), parts along dimension 0
- resp_value_grad: float32 [32, 512, 512], P(('prompt', 'resp'), None, 'head'), parts along dimension 0
- prefix_key_grad: float32 [4096, 512], P(('prompt', 'resp', 'head')), parts along dimension 0
- prefix_value_grad: float32 [4096, 512], P(('prompt', 'resp', 'head')), parts along dimension 0
The draws below stay inside these ranges and needn't reach their ends.
There are 4 independent parts, one for each index of `prompt`. The reference program is written for one: setup_inputs(seed, part) draws one part's arguments, and reference() takes and returns one part's arrays. A program takes and returns all parts, laid end to end along the dimension named above; each array names one. Nothing has to cross between parts.
Inputs may be any that keep to these rules, and one draw needn't show every extreme that they name: `resp_len`: the 8 lengths of each prompt sum to 2560.
All inputs are finite; a program needn't handle non-finite values. No bound on the sum of `resp_len` on one device may be relied on, other than what follows from the above.
Results may differ from the reference program's by a relative error of at most 0.038.
Values may be sent and summed in bfloat16 or wider, within the bound.
A program may use at most 64 MiB of HBM per device.

```python
import math
import jax
import jax.numpy as jnp
import numpy as np
from jax import lax

QH = 64
KVH = 4
HD = 128
RLEN = 512
PROMPT_SLOTS = 1024
RESP = 8


def prefix_base(key):
    normal_base = jnp.clip(jax.random.normal(key, (PROMPT_SLOTS // 2, 2, KVH * HD), jnp.float32), -6.0, 6.0)
    leading_rows = normal_base[:, 0]
    second_rows = normal_base[:, 1]
    return jnp.stack([leading_rows, second_rows], axis=1).reshape(PROMPT_SLOTS, KVH * HD)


def draw_prefix_keys(key, part):
    anchors = prefix_base(key)
    return anchors.astype(jnp.bfloat16)


def draw_queries(key, part):
    key = jax.random.fold_in(key, 11)
    values = 2.5 * jnp.clip(jax.random.normal(key, (RESP, RLEN, QH * HD), jnp.float32), -6.0, 6.0)
    return values.astype(jnp.bfloat16)


def steps_of(stream_key, dims, cuts, least, high):
    factor_of = 1.0
    for position, parts in cuts:
        steps = jax.random.uniform(jax.random.fold_in(jax.random.fold_in(stream_key, 6), position), (parts,), jnp.float32, least / len(cuts), high / len(cuts))
        factor_of = factor_of * jnp.repeat(jnp.exp(steps), dims[position] // parts).reshape((-1,) + (1,) * (len(dims) - 1 - position))
    return factor_of


def length_profile(number_of, total, bound, skew):
    portions = [(1 << 20) // math.isqrt(grade ** skew) + 1 for grade in range(2, number_of + 1)]
    rest, given = total - bound - (number_of - 1), [1] * (number_of - 1)
    while rest > 0:
        candidates = [i for i in range(number_of - 1) if given[i] < bound]
        pool, left = sum([portions[i] for i in candidates]), rest
        for i in candidates:
            extra = min(bound - given[i], max(1, left * portions[i] // pool), rest)
            given[i] = given[i] + extra
            rest = rest - extra
    return np.array([bound] + given)


def ragged(rng, count, total, most, slope):
    if count == 2:
        one = jax.random.randint(rng, (), max(1, total - most), min(most, total - 1) + 1)
        return jnp.stack([one, total - one])
    lengths = jnp.asarray(length_profile(count, total, most, slope), jnp.int32)
    couples = (count - 1) // 2
    donor, sink = lengths[1:1 + 2 * couples:2], lengths[2:2 + 2 * couples:2]
    margin = jnp.minimum(donor - 1, most - sink)
    passed = jax.random.randint(jax.random.fold_in(rng, 1), (couples,), 0, 1 << 20) % (margin + 1)
    lengths = lengths.at[1:1 + 2 * couples:2].set(donor - passed).at[2:2 + 2 * couples:2].set(sink + passed)
    return lengths[jax.random.permutation(jax.random.fold_in(rng, 2), count)]


def scatter_about(key, extent, scale, reach, shards=(), kind=jnp.bfloat16):
    gain = steps_of(key, extent, shards, -0.22, 0.18) if shards else 1.0
    values = jax.random.normal(key, extent, jnp.float32) * scale * gain
    return jnp.minimum(jnp.maximum(values, -reach), reach).astype(kind)


def setup_inputs(seed: int = 0, part: int = 0) -> dict:
    streams_of = jax.random.split(jax.random.key(seed), 9)
    own_keys = jax.random.split(jax.random.fold_in(streams_of[8], part), 9)
    return {
        "queries": draw_queries(jax.random.fold_in(jax.random.fold_in(streams_of[8], part), 71), part),
        "resp_keys": scatter_about(own_keys[1], (RESP, RLEN, KVH * HD), 1.0, 6.0, ((0, 8), (2, 8))),
        "resp_values": scatter_about(own_keys[2], (RESP, RLEN, KVH * HD), 1.0, 6.0, ((0, 8), (2, 8))),
        "prefix_keys": draw_prefix_keys(jax.random.fold_in(jax.random.fold_in(streams_of[8], part), 71), part),
        "prefix_values": scatter_about(own_keys[4], (PROMPT_SLOTS, KVH * HD), 1.0, 6.0, ((0, 64),)),
        "out_grad": scatter_about(own_keys[5], (RESP, RLEN, QH * HD), 1.0, 6.0, ((0, 8), (2, 8))),
        "resp_len": ragged(own_keys[6], RESP, RESP * RLEN * 5 // 8, RLEN, 2).astype(jnp.int32),
        "prefix_len": jax.random.randint(own_keys[7], (1,), PROMPT_SLOTS // 2, PROMPT_SLOTS + 1).astype(jnp.int32),
    }


def contract_rows(left, right):
    return lax.dot_general(left, right, (((0,), (0,)), ((), ())), preferred_element_type=jnp.float32)


def contract_cols(left, right):
    return lax.dot_general(left, right, (((1,), (1,)), ((), ())), preferred_element_type=jnp.float32)


def key_mask(row_count, prefix_rows, prefix_live, resp_live):
    row_ids = jnp.arange(row_count, dtype=jnp.int32)[:, None]
    col_ids = jnp.arange(prefix_rows + row_count, dtype=jnp.int32)[None, :]
    own_col = col_ids - prefix_rows
    in_prefix = col_ids < prefix_live
    in_resp = (own_col <= row_ids) & (own_col < resp_live)
    return jnp.where(col_ids < prefix_rows, in_prefix, in_resp)


def head_pass(query_head, grad_head, key_rows, value_rows, key_valid, row_live, score_scale):
    scores = jnp.where(key_valid, contract_cols(query_head, key_rows) * score_scale, -jnp.inf)
    row_max = jnp.max(scores, axis=1, keepdims=True)
    exp_scores = jnp.exp(scores - row_max)
    weights = exp_scores / jnp.sum(exp_scores, axis=1, keepdims=True)
    weights_low = weights.astype(jnp.bfloat16)
    mixed_rows = jnp.dot(weights_low, value_rows, preferred_element_type=jnp.float32)
    result = jnp.where(row_live, mixed_rows, 0.0).astype(jnp.bfloat16)
    grad_live = jnp.where(row_live, grad_head, jnp.zeros_like(grad_head))
    value_grad = contract_rows(weights_low, grad_live)
    weight_grad = contract_cols(grad_live, value_rows)
    centre = jnp.sum(grad_live.astype(jnp.float32) * result.astype(jnp.float32), axis=1, keepdims=True)
    score_grad = (weights * (weight_grad - centre) * score_scale).astype(jnp.bfloat16)
    query_grad = jnp.dot(score_grad, key_rows, preferred_element_type=jnp.float32).astype(jnp.bfloat16)
    key_grad = contract_rows(score_grad, query_head)
    return result, query_grad, key_grad, value_grad


def reference(queries, resp_keys, resp_values, prefix_keys, prefix_values, out_grad, resp_len, prefix_len):
    score_scale = float(HD) ** -0.5
    group_size = QH // KVH
    prefix_live = prefix_len[0]

    def one_response(running_total, items):
        prompt_key_total, prompt_value_total = running_total
        query_block, key_block, value_block, grad_block, resp_live = items
        key_all = jnp.concatenate([prefix_keys, key_block], axis=0)
        value_all = jnp.concatenate([prefix_values, value_block], axis=0)
        key_valid = key_mask(RLEN, PROMPT_SLOTS, prefix_live, resp_live)
        row_live = (jnp.arange(RLEN, dtype=jnp.int32) < resp_live)[:, None]

        def head_step(head_pos, states):
            out_rows, grad_rows, key_gradient_total, value_gradient_total = states
            kv_start = (head_pos // group_size * HD).astype(jnp.int32)
            col_start = (head_pos * HD).astype(jnp.int32)
            key_rows = lax.dynamic_slice_in_dim(key_all, kv_start, HD, 1)
            value_rows = lax.dynamic_slice_in_dim(value_all, kv_start, HD, 1)
            query_head = lax.dynamic_slice_in_dim(query_block, col_start, HD, 1)
            grad_head = lax.dynamic_slice_in_dim(grad_block, col_start, HD, 1)
            result, query_grad, key_grad, value_grad = head_pass(query_head, grad_head, key_rows, value_rows, key_valid, row_live, score_scale)
            out_rows = lax.dynamic_update_slice_in_dim(out_rows, result, col_start, 1)
            grad_rows = lax.dynamic_update_slice_in_dim(grad_rows, query_grad, col_start, 1)
            key_gradient_total = lax.dynamic_update_slice_in_dim(key_gradient_total, lax.dynamic_slice_in_dim(key_gradient_total, kv_start, HD, 1) + key_grad, kv_start, 1)
            value_gradient_total = lax.dynamic_update_slice_in_dim(value_gradient_total, lax.dynamic_slice_in_dim(value_gradient_total, kv_start, HD, 1) + value_grad, kv_start, 1)
            return (out_rows, grad_rows, key_gradient_total, value_gradient_total)

        init = (jnp.zeros((RLEN, QH * HD), jnp.bfloat16), jnp.zeros((RLEN, QH * HD), jnp.bfloat16),
                jnp.zeros((PROMPT_SLOTS + RLEN, KVH * HD), jnp.float32), jnp.zeros((PROMPT_SLOTS + RLEN, KVH * HD), jnp.float32))
        out_rows, grad_rows, key_gradient_total, value_gradient_total = lax.fori_loop(0, QH, head_step, init)
        running_total = (prompt_key_total + key_gradient_total[:PROMPT_SLOTS], prompt_value_total + value_gradient_total[:PROMPT_SLOTS])
        return running_total, (out_rows, grad_rows, key_gradient_total[PROMPT_SLOTS:], value_gradient_total[PROMPT_SLOTS:])

    begin = (jnp.zeros((PROMPT_SLOTS, KVH * HD), jnp.float32), jnp.zeros((PROMPT_SLOTS, KVH * HD), jnp.float32))
    running_total, outputs = lax.scan(one_response, begin, (queries, resp_keys, resp_values, out_grad, resp_len))
    return (outputs[0], outputs[1], outputs[2], outputs[3], running_total[0], running_total[1])
```

```python
import jax
import jax.numpy as jnp
from jax import lax
from jax.experimental import pallas as pl
from jax.experimental.pallas import tpu as pltpu
from jax.sharding import PartitionSpec as P

HD = 128
LOG2E = 1.4426950408889634
MESH = pl.DeviceIdType.MESH
F32 = jnp.float32
BF16 = jnp.bfloat16
NY = 4
NZ = 8


def contract(left, right, left_dim, right_dim):
    return lax.dot_general(
        left, right, (((left_dim,), (right_dim,)), ((), ())), preferred_element_type=F32
    )


def position():
    resp, head = lax.axis_index("resp"), lax.axis_index("head")
    core, y = lax.rem(resp, 2), lax.div(head, 2)
    z_lo = lax.rem(head, 2)
    z = resp - core + z_lo
    return core, y, z, z_lo


def device(core, y, z):
    z_lo = lax.rem(z, 2)
    return {"resp": z - z_lo + core, "head": y * 2 + z_lo}


def signal(sem, where):
    pl.semaphore_signal(sem, inc=1, device_id=where, device_id_type=MESH)


def swing(middle, step):
    return middle + (1 - 2 * (step % 2)) * ((step + 1) // 2)


HEADS = 8
ROWS = 512
HALF = ROWS // 2
PREFIX = 1024
SIDE = PREFIX // 2
TOTAL = PREFIX + ROWS
WIDTH = HD // 2
OTHERS = NY * NZ - 1
MASKED = -1e30
SCALE = float(HD) ** -0.5


def remote(src, dst, send_sem, recv_sem, where):
    return pltpu.make_async_remote_copy(
        src_ref=src, dst_ref=dst, send_sem=send_sem, recv_sem=recv_sem,
        device_id=where, device_id_type=MESH,
    )


def columns(at):
    return pl.ds(at * HD, HD) if isinstance(at, int) else pl.ds(pl.multiple_of(at * HD, HD), HD)


def each_head(step):
    def one(at, carry):
        step(at)
        return carry

    lax.fori_loop(0, HEADS, one, 0)


def attend_kernel(
    prefix_len, resp_len, q_hbm, g_hbm, small_hbm,
    o_ref, dq_ref, rkg_ref, rvg_ref, pkg_ref, pvg_ref,
    q_ref, g_ref, pref_ref, piece, gathered, half_out, half_in,
    ka_ref, va_ref, ko_ref, vo_ref, kt_ref, vt_ref, qa_ref,
    own_scores, gt_ref, gnt_ref, w_ref, ds_ref, dk_ref, dv_ref,
    pair_out, pair_in, sum_out, sum_in, term_out, term_in,
    load, y_send, y_recv, c_send, c_recv, h_send, h_recv,
    p_send, p_recv, r_send, r_recv, t_send, t_recv,
):
    core, y, z, z_lo = position()
    sibling = device(1 - core, y, z)
    partner = device(core, y, z + 1 - 2 * z_lo)
    lower = z_lo == 0

    ys = [lax.rem(y + dy, NY) for dy in range(NY)]
    zs = [lax.rem(z + dz, NZ) for dz in range(NZ)]
    z_los = [lax.rem(at, 2) for at in zs]
    resps = [at - low + core for at, low in zip(zs, z_los)]
    doubles = [at * 2 for at in ys]

    def peer(k):
        dy, dz = swing(NY // 2, k % NY), swing(NZ // 2, k // NY)
        return ys[dy], zs[dz], {"resp": resps[dz], "head": doubles[dy] + z_los[dz]}

    def loop(count, step):
        for k in range(count):
            step(k)

    loads = [
        pltpu.make_async_copy(src, dst, load.at[i])
        for i, (src, dst) in enumerate(
            [
                (small_hbm.at[2 * WIDTH :], pref_ref),
                (small_hbm.at[: 2 * WIDTH], half_out),
            ]
            + [(q_hbm.at[:, columns(at)], q_ref.at[at]) for at in range(HEADS)]
            + [(g_hbm.at[:, columns(at)], g_ref.at[at]) for at in range(HEADS)]
        )
    ]
    for copy in loads:
        copy.start()
    barrier = pltpu.get_barrier_semaphore()

    def greet(k):
        signal(barrier, peer(k)[2])

    loop(OTHERS, greet)
    signal(barrier, sibling)
    loads[0].wait()
    for other in range(NY):
        cols = slice(other * HD, (other + 1) * HD)
        piece[other, 0] = pref_ref[:16, cols]
        piece[other, 1] = pref_ref[16:, cols]
    loads[1].wait()
    pl.semaphore_wait(barrier, OTHERS + 1)

    half_copy = remote(half_out, half_in, h_send, h_recv, partner)
    half_copy.start()

    def gather_copy(k):
        to_y, to_z, where = peer(k)
        return remote(
            piece.at[to_y], gathered.at[0, z, y], y_send.at[k], y_recv.at[k], where,
        )

    loop(OTHERS, lambda k: gather_copy(k).start())
    gathered[0, z, y] = piece[y]

    live = lax.broadcasted_iota(jnp.int32, (ROWS, HD), 0) < resp_len[0]
    for copy in loads[2:]:
        copy.wait()
    for at in range(HEADS):
        live_grad = jnp.where(live, g_ref[at].astype(F32), 0.0)
        gt_ref[at] = jnp.transpose(live_grad).astype(BF16)
        w_ref[PREFIX + HALF :, at * ROWS : at * ROWS + HALF] = jnp.zeros((HALF, HALF), BF16)
        ds_ref[PREFIX + HALF :, at * ROWS : at * ROWS + HALF] = jnp.zeros((HALF, HALF), BF16)
    lane = lax.broadcasted_iota(jnp.int32, (ROWS, HD), 1)
    dk_ref[...] = jnp.zeros_like(dk_ref)
    dv_ref[...] = jnp.zeros_like(dv_ref)
    qa_ref[...] = jnp.where(lane == 0, 1.0, 0.0).astype(BF16)

    half_copy.wait_recv()
    for i, (ref, t_ref) in enumerate(((ko_ref, kt_ref), (vo_ref, vt_ref))):
        span = slice(i * WIDTH, (i + 1) * WIDTH)
        mine, other = half_out[span], half_in[span]
        whole = jnp.concatenate(
            [jnp.where(lower, mine, other), jnp.where(lower, other, mine)], axis=0
        )
        t_ref[:, PREFIX:] = whole
        ref[...] = jnp.transpose(whole.astype(F32)).astype(BF16)

    def head_lanes(at):
        start = pl.multiple_of(at * ROWS, ROWS)
        return pl.ds(start, ROWS), pl.ds(pl.multiple_of(start + HALF, HALF), HALF)

    def own_pass(at):
        q = q_ref[at]
        key_id = lax.broadcasted_iota(jnp.int32, (HALF, HALF), 0)
        row_id = lax.broadcasted_iota(jnp.int32, (HALF, HALF), 1)
        causal = key_id <= row_id
        first = contract(ko_ref[:HALF], q, 1, 1)
        own_scores[at, :HALF, :HALF] = jnp.where(causal, first[:, :HALF], MASKED)
        own_scores[at, :HALF, HALF:] = first[:, HALF:]
        second = contract(ko_ref[HALF:], q[HALF:], 1, 1)
        own_scores[at, HALF:, HALF:] = jnp.where(causal, second, MASKED)

    each_head(own_pass)

    def forward_copy(group):
        source = zs[(NZ - swing(NZ // 2, group)) % NZ]
        return remote(
            gathered.at[0, source], gathered.at[1, source], c_send.at[group], c_recv.at[group],
            sibling,
        )

    def forward(step):
        group = NZ - 1 - step

        def arrive(i):
            if group * NY + i < OTHERS:
                gather_copy(group * NY + i).wait_recv()

        loop(NY, arrive)
        forward_copy(group).start()

    loop(NZ, forward)
    index = lax.broadcasted_iota(jnp.int32, (PREFIX, HD), 0)
    key_core = core ^ (index >> 9)
    key_z = (index >> 6) & 7
    key_y = (index >> 4) & 3
    key_row = ((((key_z >> 1) * 2 + key_core) * 8 + key_y * 2 + (key_z & 1)) << 4) + (index & 15)
    key_lane = lax.broadcasted_iota(jnp.int32, (PREFIX, HD), 1)
    ka_ref[:, HD:] = jnp.where(
        (key_lane == 0) & (key_row >= prefix_len[0]), MASKED, 0.0
    ).astype(BF16)
    loop(NZ, lambda group: forward_copy(group).wait_recv())
    keys = gathered[:, :, :, 0].reshape(PREFIX, HD)
    values = gathered[:, :, :, 1].reshape(PREFIX, HD)
    ka_ref[:, :HD] = keys
    va_ref[...] = values
    vt_ref[:, :PREFIX] = jnp.transpose(values.astype(F32)).astype(BF16)

    live_row = lax.broadcasted_iota(jnp.int32, (1, ROWS), 1) < resp_len[0]
    near, far = PREFIX, PREFIX + HALF

    def fold(op, p, a, b):
        both = op(p, a)
        return jnp.concatenate([both[:, :HALF], op(both[:, HALF:], b)], axis=1)

    def prefix_pass(at):
        q = q_ref[at]
        lanes, late = head_lanes(at)
        s_p = contract(ka_ref[...], jnp.concatenate([q, qa_ref[...]], axis=1), 1, 1)
        s_a = own_scores[at, :HALF, :]
        s_b = own_scores[at, HALF:, HALF:]
        top = fold(
            jnp.maximum, jnp.max(s_p, axis=0, keepdims=True),
            jnp.max(s_a, axis=0, keepdims=True), jnp.max(s_b, axis=0, keepdims=True),
        )
        e_p = jnp.exp2((s_p - top) * (SCALE * LOG2E))
        e_a = jnp.exp2((s_a - top) * (SCALE * LOG2E))
        e_b = jnp.exp2((s_b - top[:, HALF:]) * (SCALE * LOG2E))
        inverse = 1.0 / fold(
            jnp.add, jnp.sum(e_p, axis=0, keepdims=True),
            jnp.sum(e_a, axis=0, keepdims=True), jnp.sum(e_b, axis=0, keepdims=True),
        )
        low_p, low_a, low_b = e_p.astype(BF16), e_a.astype(BF16), e_b.astype(BF16)
        w_ref[:SIDE, lanes] = low_p[:SIDE]
        w_ref[near:far, lanes] = low_a
        w_ref[far:, late] = low_b
        out = contract(vt_ref[:, :near], low_p, 1, 0) + contract(vt_ref[:, near:far], low_a, 1, 0)
        out_b = contract(vt_ref[:, far:], low_b, 1, 0)
        out = jnp.concatenate([out[:, :HALF], out[:, HALF:] + out_b], axis=1)
        out = jnp.where(live_row, out * inverse, 0.0).astype(BF16).astype(F32)
        o_ref[:, columns(at)] = jnp.transpose(out).astype(BF16)
        grad = (gt_ref[at].astype(F32) * inverse).astype(BF16)
        gnt_ref[at] = grad
        centre = jnp.sum(grad.astype(F32) * out, axis=0, keepdims=True)
        d_p = contract(va_ref[...], grad, 1, 0)
        d_a = contract(vo_ref[:HALF], grad, 1, 0)
        d_b = contract(vo_ref[HALF:], grad[:, HALF:], 1, 0)
        score_grad = (e_p * (d_p - centre)).astype(BF16)
        ds_ref[:near, lanes] = score_grad
        ds_ref[near:far, lanes] = (e_a * (d_a - centre)).astype(BF16)
        ds_ref[far:, late] = (e_b * (d_b - centre[:, HALF:])).astype(BF16)
        dk_ref[...] += contract(score_grad[SIDE:], q, 1, 0)
        dv_ref[...] += contract(low_p[SIDE:], grad, 1, 1)

    each_head(prefix_pass)

    pair_copy = remote(pair_out, pair_in, p_send, p_recv, sibling)

    def sum_copy(k):
        to_y, to_z, where = peer(k)
        return remote(
            sum_out.at[to_z, to_y], sum_in.at[z, y], r_send.at[k], r_recv.at[k], where,
        )

    term_copy = remote(term_out, term_in, t_send, t_recv, partner)

    pair_out[0] = (dk_ref[...] * SCALE).astype(BF16)
    pair_out[1] = dv_ref[...].astype(BF16)
    pair_copy.start()

    def key_block(step, carry):
        rows = pl.ds(pl.multiple_of(step * PREFIX, SIDE), SIDE)
        dk_ref[...] = jnp.zeros_like(dk_ref)
        dv_ref[...] = jnp.zeros_like(dv_ref)

        def two_heads(i, carry):
            lanes = pl.ds(pl.multiple_of(i * 2 * ROWS, 2 * ROWS), 2 * ROWS)
            pick = pl.ds(i * 2, 2)
            dk_ref[...] += contract(ds_ref[rows, lanes], q_ref[pick].reshape(2 * ROWS, HD), 1, 0)
            grads = jnp.concatenate([gnt_ref[i * 2], gnt_ref[i * 2 + 1]], axis=1)
            dv_ref[...] += contract(w_ref[rows, lanes], grads, 1, 1)
            return carry

        lax.fori_loop(0, HEADS // 2, two_heads, 0)
        dk_ref[...] *= SCALE

        @pl.when(step == 0)
        def _():
            pair_copy.wait_recv()
            for i, ref in enumerate((dk_ref, dv_ref)):
                total = ref[...] + pair_in[i].astype(F32)
                sum_out[:, :, i] = total.astype(BF16).reshape(NZ, NY, 16, HD)
            loop(OTHERS, lambda k: sum_copy(k).start())
            sum_in[z, y] = sum_out[z, y]

        return carry

    lax.fori_loop(0, 2, key_block, 0)
    for i, (ref, out_ref) in enumerate(((dk_ref, rkg_ref), (dv_ref, rvg_ref))):
        term = jnp.transpose(ref[...])
        out_ref[...] = jnp.where(lower, term[:WIDTH], term[WIDTH:])
        term_out[i] = jnp.where(lower, term[WIDTH:], term[:WIDTH]).astype(BF16)
    term_copy.start()
    kt_ref[:, :PREFIX] = jnp.transpose(ka_ref[:, :HD].astype(F32)).astype(BF16)

    def out_pass(at):
        cols = columns(at)
        lanes, late = head_lanes(at)

        def rows_of(t_ref, big_ref):
            both = contract(t_ref[:, : PREFIX + HALF], big_ref[: PREFIX + HALF, lanes], 1, 0)
            tail = contract(t_ref[:, PREFIX + HALF :], big_ref[PREFIX + HALF :, late], 1, 0)
            return jnp.concatenate([both[:, :HALF], both[:, HALF:] + tail], axis=1)

        dq_ref[:, cols] = jnp.transpose(rows_of(kt_ref, ds_ref) * SCALE).astype(BF16)

    each_head(out_pass)

    term_copy.wait_recv()
    rkg_ref[...] += term_in[0].astype(F32)
    rvg_ref[...] += term_in[1].astype(F32)
    loop(OTHERS, lambda k: sum_copy(k).wait_recv())
    for y_at in range(NY):
        cols = slice(y_at * HD, (y_at + 1) * HD)
        total = jnp.sum(sum_in[:, y_at].astype(F32), axis=0)
        pkg_ref[:, cols] = total[0]
        pvg_ref[:, cols] = total[1]
    def drain(k):
        gather_copy(k).wait_send()
        sum_copy(k).wait_send()

    loop(OTHERS, drain)
    loop(NZ, lambda group: forward_copy(group).wait_send())
    for copy in (half_copy, pair_copy, term_copy):
        copy.wait_send()


def attend(prefix_len, resp_len, queries, out_grad, small):
    vmem = pl.BlockSpec(memory_space=pltpu.VMEM)
    smem = pl.BlockSpec(memory_space=pltpu.SMEM)
    anywhere = pl.BlockSpec(memory_space=pl.ANY)
    dma = pltpu.SemaphoreType.DMA
    return pl.pallas_call(
        attend_kernel,
        out_shape=[
            jax.ShapeDtypeStruct((ROWS, HEADS * HD), BF16),
            jax.ShapeDtypeStruct((ROWS, HEADS * HD), BF16),
            jax.ShapeDtypeStruct((WIDTH, ROWS), F32),
            jax.ShapeDtypeStruct((WIDTH, ROWS), F32),
            jax.ShapeDtypeStruct((16, NY * HD), F32),
            jax.ShapeDtypeStruct((16, NY * HD), F32),
        ],
        in_specs=[smem] * 2 + [anywhere] * 3,
        out_specs=[vmem] * 6,
        scratch_shapes=[
            pltpu.VMEM((HEADS, ROWS, HD), BF16),
            pltpu.VMEM((HEADS, ROWS, HD), BF16),
            pltpu.VMEM((32, NY * HD), BF16),
            pltpu.VMEM((NY, 2, 16, HD), BF16),
            pltpu.VMEM((2, NZ, NY, 2, 16, HD), BF16),
            pltpu.VMEM((2 * WIDTH, ROWS), BF16),
            pltpu.VMEM((2 * WIDTH, ROWS), BF16),
            pltpu.VMEM((PREFIX, 2 * HD), BF16),
            pltpu.VMEM((PREFIX, HD), BF16),
            pltpu.VMEM((ROWS, HD), BF16),
            pltpu.VMEM((ROWS, HD), BF16),
            pltpu.VMEM((HD, TOTAL), BF16),
            pltpu.VMEM((HD, TOTAL), BF16),
            pltpu.VMEM((ROWS, HD), BF16),
            pltpu.VMEM((HEADS, ROWS, ROWS), F32),
            pltpu.VMEM((HEADS, HD, ROWS), BF16),
            pltpu.VMEM((HEADS, HD, ROWS), BF16),
            pltpu.VMEM((TOTAL, HEADS * ROWS), BF16),
            pltpu.VMEM((TOTAL, HEADS * ROWS), BF16),
            pltpu.VMEM((SIDE, HD), F32),
            pltpu.VMEM((SIDE, HD), F32),
            pltpu.VMEM((2, SIDE, HD), BF16),
            pltpu.VMEM((2, SIDE, HD), BF16),
            pltpu.VMEM((NZ, NY, 2, 16, HD), BF16),
            pltpu.VMEM((NZ, NY, 2, 16, HD), BF16),
            pltpu.VMEM((2, WIDTH, ROWS), BF16),
            pltpu.VMEM((2, WIDTH, ROWS), BF16),
            dma((2 + 2 * HEADS,)),
            dma((OTHERS,)), dma((OTHERS,)), dma((NZ,)), dma((NZ,)), dma, dma,
            dma, dma, dma((OTHERS,)), dma((OTHERS,)), dma, dma,
        ],
        compiler_params=pltpu.CompilerParams(
            collective_id=0, has_side_effects=True, vmem_limit_bytes=51 * 2**20
        ),
        name="attend",
    )(prefix_len, resp_len, queries, out_grad, small)


def finish_kernel(*refs):
    count = len(refs) // 2
    sems = refs[-1]
    copies = [
        pltpu.make_async_copy(refs[i], refs[count + i], sems.at[i]) for i in range(count)
    ]
    for copy in copies:
        copy.start()
    for copy in copies:
        copy.wait()


def finish(arrays):
    vmem = pl.BlockSpec(memory_space=pltpu.VMEM)
    anywhere = pl.BlockSpec(memory_space=pl.ANY)
    return pl.pallas_call(
        finish_kernel,
        out_shape=[jax.ShapeDtypeStruct(a.shape, a.dtype) for a in arrays],
        in_specs=[vmem] * len(arrays),
        out_specs=[anywhere] * len(arrays),
        scratch_shapes=[pltpu.SemaphoreType.DMA((len(arrays),))],
        compiler_params=pltpu.CompilerParams(vmem_limit_bytes=8 * 2**20),
        name="finish",
    )(*arrays)


def body(
    queries, resp_keys, resp_values, prefix_keys, prefix_values, out_grad, resp_len, prefix_len
):
    small = jnp.concatenate(
        [
            jnp.swapaxes(resp_keys[0], 0, 1), jnp.swapaxes(resp_values[0], 0, 1),
            prefix_keys, prefix_values,
        ],
        axis=0,
    )
    results = attend(prefix_len, resp_len, queries[0], out_grad[0], small)
    attn_out, query_grad, rkg, rvg, pkg, pvg = finish(results)
    return (
        attn_out[None],
        query_grad[None],
        jnp.swapaxes(rkg, 0, 1)[None],
        jnp.swapaxes(rvg, 0, 1)[None],
        pkg,
        pvg,
    )


def solution(mesh):
    in_specs = (
        P(("prompt", "resp"), None, "head"),
        P(("prompt", "resp"), None, "head"),
        P(("prompt", "resp"), None, "head"),
        P(("prompt", "resp", "head"), None),
        P(("prompt", "resp", "head"), None),
        P(("prompt", "resp"), None, "head"),
        P(("prompt", "resp")),
        P("prompt"),
    )
    out_specs = (
        P(("prompt", "resp"), None, "head"),
        P(("prompt", "resp"), None, "head"),
        P(("prompt", "resp"), None, "head"),
        P(("prompt", "resp"), None, "head"),
        P(("prompt", "resp", "head"), None),
        P(("prompt", "resp", "head"), None),
    )
    return jax.shard_map(body, mesh=mesh, in_specs=in_specs, out_specs=out_specs, check_vma=False)
```

```python
import jax
import jax.numpy as jnp
from jax import lax
from jax.experimental import pallas as pl
from jax.experimental.pallas import tpu as pltpu
from jax.sharding import PartitionSpec as P

HD = 128
LOG2E = 1.4426950408889634
MESH = pl.DeviceIdType.MESH
F32 = jnp.float32
BF16 = jnp.bfloat16
NY = 4
NZ = 8


def contract(left, right, left_dim, right_dim):
    return lax.dot_general(
        left, right, (((left_dim,), (right_dim,)), ((), ())), preferred_element_type=F32
    )


def position():
    resp, head = lax.axis_index("resp"), lax.axis_index("head")
    core, y = lax.rem(resp, 2), lax.div(head, 2)
    z_lo = lax.rem(head, 2)
    z = resp - core + z_lo
    return core, y, z, z_lo


def device(core, y, z):
    z_lo = lax.rem(z, 2)
    return {"resp": z - z_lo + core, "head": y * 2 + z_lo}


def signal(sem, where):
    pl.semaphore_signal(sem, inc=1, device_id=where, device_id_type=MESH)


def swing(middle, step):
    return middle + (1 - 2 * (step % 2)) * ((step + 1) // 2)


HEADS = 8
ROWS = 512
HALF = ROWS // 2
WIDE = 4 * ROWS
PREFIX = 1024
SIDE = PREFIX // 2
TOTAL = PREFIX + ROWS
WIDTH = HD // 2
OTHERS = NY * NZ - 1
MASKED = -1e30
SCALE = float(HD) ** -0.5


def remote(src, dst, send_sem, recv_sem, where):
    return pltpu.make_async_remote_copy(
        src_ref=src, dst_ref=dst, send_sem=send_sem, recv_sem=recv_sem,
        device_id=where, device_id_type=MESH,
    )


def columns(at):
    return pl.ds(at * HD, HD) if isinstance(at, int) else pl.ds(pl.multiple_of(at * HD, HD), HD)


def each_head(step, begin=0, end=HEADS):
    def one(at, carry):
        step(at)
        return carry

    lax.fori_loop(begin, end, one, 0)


def attend_kernel(
    prefix_len, resp_len, q_hbm, g_hbm, small_hbm,
    o_ref, dq_ref, rkg_ref, rvg_ref, pkg_ref, pvg_ref,
    q_ref, g_ref, pref_ref, piece, gathered, half_out, half_in,
    ka_ref, va_ref, ko_ref, vo_ref, kt_ref, vt_ref, qa_ref,
    own_out, mix_ref, stats, gt_ref, gnt_ref, w_ref, ds_ref, dk_ref, dv_ref,
    pair_out, pair_in, sum_out, sum_in, term_out, term_in,
    load, y_send, y_recv, c_send, c_recv, h_send, h_recv,
    p_send, p_recv, r_send, r_recv, t_send, t_recv,
):
    core, y, z, z_lo = position()
    sibling = device(1 - core, y, z)
    partner = device(core, y, z + 1 - 2 * z_lo)
    lower = z_lo == 0

    ys = [lax.rem(y + dy, NY) for dy in range(NY)]
    zs = [lax.rem(z + dz, NZ) for dz in range(NZ)]
    z_los = [lax.rem(at, 2) for at in zs]
    resps = [at - low + core for at, low in zip(zs, z_los)]
    doubles = [at * 2 for at in ys]

    def peer(k):
        dy, dz = swing(NY // 2, k % NY), swing(NZ // 2, k // NY)
        return ys[dy], zs[dz], {"resp": resps[dz], "head": doubles[dy] + z_los[dz]}

    def loop(count, step):
        for k in range(count):
            step(k)

    loads = [
        pltpu.make_async_copy(src, dst, load.at[i])
        for i, (src, dst) in enumerate(
            [
                (small_hbm.at[2 * WIDTH :], pref_ref),
                (small_hbm.at[: 2 * WIDTH], half_out),
            ]
            + [(q_hbm.at[:, columns(at)], q_ref.at[at]) for at in range(HEADS)]
            + [(g_hbm.at[:, columns(at)], g_ref.at[at]) for at in range(HEADS)]
        )
    ]
    for copy in loads:
        copy.start()
    barrier = pltpu.get_barrier_semaphore()

    def greet(k):
        signal(barrier, peer(k)[2])

    loop(OTHERS, greet)
    signal(barrier, sibling)
    loads[0].wait()
    for other in range(NY):
        cols = slice(other * HD, (other + 1) * HD)
        piece[other, 0] = pref_ref[:16, cols]
        piece[other, 1] = pref_ref[16:, cols]
    loads[1].wait()
    pl.semaphore_wait(barrier, OTHERS + 1)

    half_copy = remote(half_out, half_in, h_send, h_recv, partner)
    half_copy.start()

    def gather_copy(k):
        to_y, to_z, where = peer(k)
        return remote(
            piece.at[to_y], gathered.at[0, z, y], y_send, y_recv.at[k], where,
        )

    loop(OTHERS, lambda k: gather_copy(k).start())
    gathered[0, z, y] = piece[y]

    live = lax.broadcasted_iota(jnp.int32, (ROWS, HD), 0) < resp_len[0]
    for copy in loads[2:]:
        copy.wait()
    for at in range(HEADS):
        live_grad = jnp.where(live, g_ref[at].astype(F32), 0.0)
        gt_ref[:, at * ROWS : (at + 1) * ROWS] = jnp.transpose(live_grad).astype(BF16)
        w_ref[SIDE + HALF :, at * ROWS : at * ROWS + HALF] = jnp.zeros((HALF, HALF), BF16)
    lane = lax.broadcasted_iota(jnp.int32, (ROWS, HD), 1)
    dk_ref[...] = jnp.zeros_like(dk_ref)
    dv_ref[...] = jnp.zeros_like(dv_ref)
    qa_ref[...] = jnp.where(lane == 0, 1.0, 0.0).astype(BF16)

    half_copy.wait_recv()
    for i, (ref, t_ref) in enumerate(((ko_ref, kt_ref), (vo_ref, vt_ref))):
        span = slice(i * WIDTH, (i + 1) * WIDTH)
        mine, other = half_out[span], half_in[span]
        whole = jnp.concatenate(
            [jnp.where(lower, mine, other), jnp.where(lower, other, mine)], axis=0
        )
        t_ref[:, PREFIX:] = whole
        ref[...] = jnp.transpose(whole.astype(F32)).astype(BF16)

    def head_lanes(at):
        start = pl.multiple_of(at * ROWS, ROWS)
        return pl.ds(start, ROWS), pl.ds(pl.multiple_of(start + HALF, HALF), HALF)

    near, far = PREFIX, PREFIX + HALF

    def fold(op, a, b):
        return jnp.concatenate([a[:, :HALF], op(a[:, HALF:], b)], axis=1)

    def own_pass(at):
        q = q_ref[at]
        key_id = lax.broadcasted_iota(jnp.int32, (HALF, HALF), 0)
        row_id = lax.broadcasted_iota(jnp.int32, (HALF, HALF), 1)
        causal = key_id <= row_id
        lanes, late = head_lanes(at)
        first = contract(ko_ref[:HALF], q, 1, 1)
        s_a = jnp.concatenate(
            [jnp.where(causal, first[:, :HALF], MASKED), first[:, HALF:]], axis=1
        )
        s_b = jnp.where(causal, contract(ko_ref[HALF:], q[HALF:], 1, 1), MASKED)
        top = fold(jnp.maximum, jnp.max(s_a, axis=0, keepdims=True), jnp.max(s_b, axis=0, keepdims=True))
        e_a = jnp.exp2((s_a - top) * (SCALE * LOG2E))
        e_b = jnp.exp2((s_b - top[:, HALF:]) * (SCALE * LOG2E))
        stats[0:1, lanes] = top
        stats[1:2, lanes] = fold(
            jnp.add, jnp.sum(e_a, axis=0, keepdims=True), jnp.sum(e_b, axis=0, keepdims=True)
        )
        low_a, low_b = e_a.astype(BF16), e_b.astype(BF16)
        w_ref[SIDE : SIDE + HALF, lanes] = low_a
        w_ref[SIDE + HALF :, late] = low_b
        own_out[:, lanes] = fold(
            jnp.add,
            contract(vt_ref[:, near:far], low_a, 1, 0), contract(vt_ref[:, far:], low_b, 1, 0),
        )

    each_head(own_pass, 0, 5)

    def forward_copy(group):
        source = zs[(NZ - swing(NZ // 2, group)) % NZ]
        return remote(
            gathered.at[0, source], gathered.at[1, source], c_send.at[group], c_recv.at[group],
            sibling,
        )

    def forward(step):
        group = NZ - 1 - step

        def arrive(i):
            if group * NY + i < OTHERS:
                gather_copy(group * NY + i).wait_recv()

        loop(NY, arrive)
        forward_copy(group).start()

    loop(NZ, forward)

    def take(side):
        rows = slice(side * SIDE, (side + 1) * SIDE)
        values = gathered[side, :, :, 1].reshape(SIDE, HD)
        ka_ref[rows, :HD] = gathered[side, :, :, 0].reshape(SIDE, HD)
        va_ref[rows] = values
        vt_ref[:, rows] = jnp.transpose(values.astype(F32)).astype(BF16)

    take(0)
    each_head(own_pass, 5, HEADS)
    index = lax.broadcasted_iota(jnp.int32, (PREFIX, HD), 0)
    key_core = core ^ (index >> 9)
    key_z = (index >> 6) & 7
    key_y = (index >> 4) & 3
    key_row = ((((key_z >> 1) * 2 + key_core) * 8 + key_y * 2 + (key_z & 1)) << 4) + (index & 15)
    key_lane = lax.broadcasted_iota(jnp.int32, (PREFIX, HD), 1)
    ka_ref[:, HD:] = jnp.where(
        (key_lane == 0) & (key_row >= prefix_len[0]), MASKED, 0.0
    ).astype(BF16)
    loop(NZ, lambda group: forward_copy(group).wait_recv())

    take(1)
    lane_row = lax.broadcasted_iota(jnp.int32, (1, WIDE), 1) & (ROWS - 1)
    live_row = lane_row < resp_len[0]

    def prefix_pass(at):
        heads = WIDE // ROWS
        q = q_ref[pl.ds(at * heads, heads)].reshape(WIDE, HD)
        lanes = pl.ds(pl.multiple_of(at * WIDE, WIDE), WIDE)
        ones = jnp.concatenate([qa_ref[...]] * heads, axis=0)
        s_p = contract(ka_ref[...], jnp.concatenate([q, ones], axis=1), 1, 1)
        own_top = stats[0:1, lanes]
        top = jnp.maximum(jnp.max(s_p, axis=0, keepdims=True), own_top)
        e_p = jnp.exp2((s_p - top) * (SCALE * LOG2E))
        share = jnp.exp2((own_top - top) * (SCALE * LOG2E))
        inverse = 1.0 / (jnp.sum(e_p, axis=0, keepdims=True) + share * stats[1:2, lanes])
        low_p = e_p.astype(BF16)
        w_ref[:SIDE, lanes] = low_p[:SIDE]
        out = contract(vt_ref[:, :near], low_p, 1, 0) + share * own_out[:, lanes]
        out = jnp.where(live_row, out * inverse, 0.0).astype(BF16)
        mix_ref[:, lanes] = out
        grad = (gt_ref[:, lanes].astype(F32) * inverse).astype(BF16)
        gnt_ref[:, lanes] = grad
        centre = jnp.sum(grad.astype(F32) * out.astype(F32), axis=0, keepdims=True)
        d_p = contract(va_ref[...], grad, 1, 0)
        stats[2:3, lanes] = share * inverse
        stats[3:4, lanes] = share * centre
        score_grad = (e_p * (d_p - centre)).astype(BF16)
        ds_ref[:near, lanes] = score_grad
        dk_ref[...] += contract(score_grad[SIDE:], q, 1, 0)
        dv_ref[...] += contract(low_p[SIDE:], grad, 1, 1)

    each_head(prefix_pass, 0, HEADS * ROWS // WIDE)

    pair_copy = remote(pair_out, pair_in, p_send, p_recv, sibling)

    def sum_copy(k):
        to_y, to_z, where = peer(k)
        return remote(
            sum_out.at[to_z * NY + to_y], sum_in.at[z * NY + y], r_send, r_recv, where,
        )

    term_copy = remote(term_out, term_in, t_send, t_recv, partner)

    pair_out[0] = (dk_ref[...] * SCALE).astype(BF16)
    pair_out[1] = dv_ref[...].astype(BF16)
    pair_copy.start()

    dk_ref[...] = jnp.zeros_like(dk_ref)
    dv_ref[...] = jnp.zeros_like(dv_ref)

    def two_heads(i):
        lanes = pl.ds(pl.multiple_of(i * 2 * ROWS, 2 * ROWS), 2 * ROWS)
        q = q_ref[pl.ds(i * 2, 2)].reshape(2 * ROWS, HD)
        dk_ref[...] += contract(ds_ref[:SIDE, lanes], q, 1, 0)
        dv_ref[...] += contract(w_ref[:SIDE, lanes], gnt_ref[:, lanes], 1, 1)

    each_head(two_heads, 0, HEADS // 2)
    pair_copy.wait_recv()
    for i, (ref, factor) in enumerate(((dk_ref, SCALE), (dv_ref, 1.0))):
        total = ref[...] * factor + pair_in[i].astype(F32)
        sum_out[:, i] = total.astype(BF16).reshape(NZ * NY, 16, HD)
    loop(OTHERS, lambda k: sum_copy(k).start())
    sum_in[z * NY + y] = sum_out[z * NY + y]
    others = pl.ds(0, OTHERS)
    all_gathers = remote(sum_out.at[others], sum_in.at[others], y_send, r_recv, sibling)
    all_sums = remote(sum_out.at[others], sum_in.at[others], r_send, r_recv, sibling)
    all_gathers.wait_send()
    loop(NZ, lambda group: forward_copy(group).wait_send())
    half_copy.wait_send()
    pair_copy.wait_send()

    dk_ref[...] = jnp.zeros_like(dk_ref)
    dv_ref[...] = jnp.zeros_like(dv_ref)

    def own_grad_pass(at):
        lanes = pl.ds(pl.multiple_of(at * WIDE, WIDE), WIDE)
        q = q_ref[pl.ds(at * (WIDE // ROWS), WIDE // ROWS)].reshape(WIDE, HD)
        grad = (gt_ref[:, lanes].astype(F32) * stats[2:3, lanes]).astype(BF16)
        low = w_ref[SIDE:, lanes]
        weight_grad = contract(vo_ref[...], grad, 1, 0)
        score_grad = (low.astype(F32) * (weight_grad - stats[3:4, lanes])).astype(BF16)
        ds_ref[near:, lanes] = score_grad
        dk_ref[...] += contract(score_grad, q, 1, 0)
        dv_ref[...] += contract(low, grad, 1, 1)

    each_head(own_grad_pass, 0, HEADS * ROWS // WIDE)
    dk_ref[...] *= SCALE
    for i, (ref, out_ref) in enumerate(((dk_ref, rkg_ref), (dv_ref, rvg_ref))):
        term = jnp.transpose(ref[...])
        out_ref[...] = jnp.where(lower, term[:WIDTH], term[WIDTH:])
        term_out[i] = jnp.where(lower, term[WIDTH:], term[:WIDTH]).astype(BF16)
    term_copy.start()
    kt_ref[:, :PREFIX] = jnp.transpose(ka_ref[:, :HD].astype(F32)).astype(BF16)

    def out_pass(at):
        heads = 4
        lanes = pl.ds(pl.multiple_of(at * heads * ROWS, heads * ROWS), heads * ROWS)
        rows = contract(kt_ref[...], ds_ref[:, lanes], 1, 0) * SCALE
        mixed = mix_ref[:, lanes].astype(F32)
        for i in range(heads):
            cols = columns(at * heads + i)
            span = slice(i * ROWS, (i + 1) * ROWS)
            o_ref[:, cols] = jnp.transpose(mixed[:, span]).astype(BF16)
            dq_ref[:, cols] = jnp.transpose(rows[:, span]).astype(BF16)

    each_head(out_pass, 0, HEADS // 4)

    term_copy.wait_recv()
    rkg_ref[...] += term_in[0].astype(F32)
    rvg_ref[...] += term_in[1].astype(F32)
    all_sums.wait_recv()
    sums = sum_in[...].reshape(NZ, NY, 2, 16, HD)
    for y_at in range(NY):
        cols = slice(y_at * HD, (y_at + 1) * HD)
        total = jnp.sum(sums[:, y_at].astype(F32), axis=0)
        pkg_ref[:, cols] = total[0]
        pvg_ref[:, cols] = total[1]
    all_sums.wait_send()
    term_copy.wait_send()


def attend(prefix_len, resp_len, queries, out_grad, small):
    vmem = pl.BlockSpec(memory_space=pltpu.VMEM)
    smem = pl.BlockSpec(memory_space=pltpu.SMEM)
    anywhere = pl.BlockSpec(memory_space=pl.ANY)
    dma = pltpu.SemaphoreType.DMA
    return pl.pallas_call(
        attend_kernel,
        out_shape=[
            jax.ShapeDtypeStruct((ROWS, HEADS * HD), BF16),
            jax.ShapeDtypeStruct((ROWS, HEADS * HD), BF16),
            jax.ShapeDtypeStruct((WIDTH, ROWS), F32),
            jax.ShapeDtypeStruct((WIDTH, ROWS), F32),
            jax.ShapeDtypeStruct((16, NY * HD), F32),
            jax.ShapeDtypeStruct((16, NY * HD), F32),
        ],
        in_specs=[smem] * 2 + [anywhere] * 3,
        out_specs=[vmem] * 6,
        scratch_shapes=[
            pltpu.VMEM((HEADS, ROWS, HD), BF16),
            pltpu.VMEM((HEADS, ROWS, HD), BF16),
            pltpu.VMEM((32, NY * HD), BF16),
            pltpu.VMEM((NY, 2, 16, HD), BF16),
            pltpu.VMEM((2, NZ, NY, 2, 16, HD), BF16),
            pltpu.VMEM((2 * WIDTH, ROWS), BF16),
            pltpu.VMEM((2 * WIDTH, ROWS), BF16),
            pltpu.VMEM((PREFIX, 2 * HD), BF16),
            pltpu.VMEM((PREFIX, HD), BF16),
            pltpu.VMEM((ROWS, HD), BF16),
            pltpu.VMEM((ROWS, HD), BF16),
            pltpu.VMEM((HD, TOTAL), BF16),
            pltpu.VMEM((HD, TOTAL), BF16),
            pltpu.VMEM((ROWS, HD), BF16),
            pltpu.VMEM((HD, HEADS * ROWS), F32),
            pltpu.VMEM((HD, HEADS * ROWS), BF16),
            pltpu.VMEM((8, HEADS * ROWS), F32),
            pltpu.VMEM((HD, HEADS * ROWS), BF16),
            pltpu.VMEM((HD, HEADS * ROWS), BF16),
            pltpu.VMEM((SIDE + ROWS, HEADS * ROWS), BF16),
            pltpu.VMEM((TOTAL, HEADS * ROWS), BF16),
            pltpu.VMEM((SIDE, HD), F32),
            pltpu.VMEM((SIDE, HD), F32),
            pltpu.VMEM((2, SIDE, HD), BF16),
            pltpu.VMEM((2, SIDE, HD), BF16),
            pltpu.VMEM((NZ * NY, 2, 16, HD), BF16),
            pltpu.VMEM((NZ * NY, 2, 16, HD), BF16),
            pltpu.VMEM((2, WIDTH, ROWS), BF16),
            pltpu.VMEM((2, WIDTH, ROWS), BF16),
            dma((2 + 2 * HEADS,)),
            dma, dma((OTHERS,)), dma((NZ,)), dma((NZ,)), dma, dma,
            dma, dma, dma, dma, dma, dma,
        ],
        compiler_params=pltpu.CompilerParams(
            collective_id=0, has_side_effects=True, vmem_limit_bytes=51 * 2**20
        ),
        name="attend",
    )(prefix_len, resp_len, queries, out_grad, small)


def finish_kernel(*refs):
    count = len(refs) // 2
    sems = refs[-1]
    copies = [
        pltpu.make_async_copy(refs[i], refs[count + i], sems.at[i]) for i in range(count)
    ]
    for copy in copies:
        copy.start()
    for copy in copies:
        copy.wait()


def finish(arrays):
    vmem = pl.BlockSpec(memory_space=pltpu.VMEM)
    anywhere = pl.BlockSpec(memory_space=pl.ANY)
    return pl.pallas_call(
        finish_kernel,
        out_shape=[jax.ShapeDtypeStruct(a.shape, a.dtype) for a in arrays],
        in_specs=[vmem] * len(arrays),
        out_specs=[anywhere] * len(arrays),
        scratch_shapes=[pltpu.SemaphoreType.DMA((len(arrays),))],
        compiler_params=pltpu.CompilerParams(vmem_limit_bytes=8 * 2**20),
        name="finish",
    )(*arrays)


def body(
    queries, resp_keys, resp_values, prefix_keys, prefix_values, out_grad, resp_len, prefix_len
):
    small = jnp.concatenate(
        [
            jnp.swapaxes(resp_keys[0], 0, 1), jnp.swapaxes(resp_values[0], 0, 1),
            prefix_keys, prefix_values,
        ],
        axis=0,
    )
    results = attend(prefix_len, resp_len, queries[0], out_grad[0], small)
    attn_out, query_grad, rkg, rvg, pkg, pvg = finish(results)
    return (
        attn_out[None],
        query_grad[None],
        jnp.swapaxes(rkg, 0, 1)[None],
        jnp.swapaxes(rvg, 0, 1)[None],
        pkg,
        pvg,
    )


def solution(mesh):
    in_specs = (
        P(("prompt", "resp"), None, "head"),
        P(("prompt", "resp"), None, "head"),
        P(("prompt", "resp"), None, "head"),
        P(("prompt", "resp", "head"), None),
        P(("prompt", "resp", "head"), None),
        P(("prompt", "resp"), None, "head"),
        P(("prompt", "resp")),
        P("prompt"),
    )
    out_specs = (
        P(("prompt", "resp"), None, "head"),
        P(("prompt", "resp"), None, "head"),
        P(("prompt", "resp"), None, "head"),
        P(("prompt", "resp"), None, "head"),
        P(("prompt", "resp", "head"), None),
        P(("prompt", "resp", "head"), None),
    )
    return jax.shard_map(body, mesh=mesh, in_specs=in_specs, out_specs=out_specs, check_vma=False)
```
